32 devices in a mesh: groups: 2 (over y), tensor: 4 (over z), vocab: 2 (over x), seq: 2 (over core).
Axes of the slice: x: 2, y: 2, z: 4, core: 2. Of those that a mesh axis runs over, the one named last changes fastest.
Arguments:
- heads_out: bfloat16 [4, 32, 1024], P(('groups', 'seq'), None, 'tensor'), parts along dimension 0, may hold values from -6 to 6
- out_weight: bfloat16 [1024, 5120], P('tensor', 'vocab'), may hold values from -0.1875 to 0.1875
- residual: bfloat16 [4, 32, 5120], P(('groups', 'seq'), 'tensor', 'vocab'), parts along dimension 0, may hold values from -32 to 32
- norm_gain: bfloat16 [5120], P('vocab'), may hold values from 0.5 to 1.5
- head_weight: bfloat16 [6144, 5120], P(('tensor', 'vocab', 'seq')), may hold values from -8 to 8
- targets: int32 [4, 32], P('groups'), parts along dimension 0, may hold values from 0 to 6143
- lengths: int32 [2], P('groups'), parts along dimension 0, may hold values from 16 to 64
Outputs:
- logprobs: float32 [4, 32], P(('groups', 'seq'), 'tensor'), parts along dimension 0
- entropies: float32 [4, 32], P(('groups', 'seq'), 'tensor'), parts along dimension 0
The draws below stay inside these ranges and needn't reach their ends.
There are 2 independent parts, one for each index of `groups`. The reference program is written for one: setup_inputs(seed, part) draws one part's arguments, and reference() takes and returns one part's arrays. A program takes and returns all parts, laid end to end along the dimension named above; an argument that names none is the same for every part. Nothing has to cross between parts.
All inputs are finite; a program needn't handle non-finite values.
Results may differ from the reference program's by a relative error of at most 0.0061.
Values may be sent and summed in bfloat16 or wider, within the bound.
A program may use at most 64 MiB of HBM per device.

```python
import math
import jax
import jax.numpy as jnp
import numpy as np
from jax import lax

D = 5120
HEAD_DIM = 128
VOC_DEV = 384
SPANS = 2
SPAN = 32
TOKENS = 64
HEADS = 8
VOCAB = 6144


def draw_residual(key, part):
    key = jax.random.fold_in(key, 11)
    keys = jax.random.split(key, 3)
    shape = (TOKENS // SPAN, SPAN, D)
    column = jnp.arange(D, dtype=jnp.float32)
    col_level = jax.random.uniform(keys[0], (D,), jnp.float32)
    row_level = jax.random.uniform(keys[1], (TOKENS // SPAN, SPAN, 1), jnp.float32)
    col_scale = jnp.power(10.0, col_level) / 4.64
    row_scale = jnp.power(10.0, row_level) / 4.64
    base = jnp.clip(jax.random.normal(keys[2], shape, jnp.float32), -6.0, 6.0)
    rise = jnp.sqrt((1.0 + 4.0 * column / D) / 3.0)
    values = base * col_scale * rise * row_scale
    return jnp.clip(values, -32.0, 32.0).astype(jnp.bfloat16)


def draw_head_weight(key, part):
    key = jax.random.fold_in(key, 23)
    keys = jax.random.split(key, 2)
    row_level = jax.random.uniform(keys[0], (VOCAB, 1), jnp.float32)
    row_scale = 0.7 * jnp.power(10.0, row_level) / jnp.sqrt(jnp.float32(D))
    base = jnp.clip(jax.random.normal(keys[1], (VOCAB, D), jnp.float32), -6.0, 6.0)
    values = base * row_scale
    return jnp.clip(values, -8.0, 8.0).astype(jnp.bfloat16)


def with_ends(result, key, least, largest):
    index_at = [jax.random.randint(jax.random.fold_in(key, axis), (), 0, length) for axis, length in enumerate(result.shape)]
    widest = result.shape.index(max(result.shape))
    beside = index_at[:widest] + [(index_at[widest] + 1) % result.shape[widest]] + index_at[widest + 1:]
    return result.at[tuple(index_at)].set(least).at[tuple(beside)].set(largest)


def with_spikes(array, own_key, source, target, shards_of, factor):
    def block_of(dim):
        return (jnp.arange(array.shape[dim]) // (array.shape[dim] // shards_of)).reshape((-1,) + (1,) * (array.ndim - 1 - dim))

    first = jax.random.permutation(own_key, shards_of)[block_of(target)]
    second = (block_of(target) + shards_of // 2) % shards_of
    return jnp.where((block_of(source) == first) | (block_of(source) == second), factor * array, array)


def levels(key, shape, pieces, low, top_value):
    def one(position, shards_of):
        steps = jax.random.uniform(jax.random.fold_in(jax.random.fold_in(key, 6), position), (shards_of,), jnp.float32, low / len(pieces), top_value / len(pieces))
        return jnp.repeat(jnp.exp(steps), shape[position] // shards_of).reshape((-1,) + (1,) * (len(shape) - position - 1))

    factor_of = one(*pieces[0])
    for cut in pieces[1:]:
        factor_of = factor_of * one(*cut)
    return factor_of


def cumulative_ranks(amount, slope):
    loads = [(1 << 20) // math.isqrt(standing ** slope) + 1 for standing in range(1, amount + 1)]
    spread = 1 + sum(loads) // (1 << 30)
    return np.cumsum(np.array([max(1, weight // spread) for weight in loads]))


def ranked_ids(rng, shape, count, slope):
    grid = cumulative_ranks(count, slope)
    pick = jax.random.randint(jax.random.fold_in(rng, 1), shape, 0, int(grid[count - 1]))
    grade = jnp.searchsorted(jnp.asarray(grid, jnp.int32), pick, side="right")
    return jax.random.permutation(jax.random.fold_in(rng, 2), count)[grade].astype(jnp.int32)


def gaussian(own_key, shape, scale, bound, cuts=(), kind=jnp.bfloat16):
    loudness = levels(own_key, shape, cuts, -0.22, 0.18) if cuts else 1.0
    drawn = jax.random.normal(own_key, shape, jnp.float32) * scale * loudness
    return jnp.minimum(jnp.maximum(drawn, -bound), bound).astype(kind)


def heavy_noise(stream_key, shape, spread, reach, cuts, heavy, held_as=jnp.bfloat16):
    result = spread * jax.random.normal(stream_key, shape, jnp.float32)
    if cuts:
        result = result * levels(stream_key, shape, cuts, -0.22, 0.18)
    return jnp.clip(with_spikes(result, jax.random.fold_in(stream_key, 3), *heavy), -reach, reach).astype(held_as)


def setup_inputs(seed: int = 0, part: int = 0) -> dict:
    key_of = jax.random.split(jax.random.key(seed), 8)
    own_keys = jax.random.split(jax.random.fold_in(key_of[7], part), 8)
    return {
        "heads_out": heavy_noise(own_keys[0], (SPANS, SPAN, HEADS * HEAD_DIM), 1.0, 6.0, ((0, 2), (2, 4)), (2, 1, 4, 2.0)),
        "out_weight": gaussian(key_of[1], (HEADS * HEAD_DIM, D), (HEADS * HEAD_DIM) ** -0.5, 0.1875, ((0, 4), (1, 2))),
        "residual": draw_residual(jax.random.fold_in(jax.random.fold_in(key_of[7], part), 71), part),
        "norm_gain": jnp.clip(1.0 + 0.1 * jax.random.normal(key_of[3], (D,), jnp.float32), 0.5, 1.5).astype(jnp.bfloat16),
        "head_weight": draw_head_weight(jax.random.fold_in(key_of[7], 71), part),
        "targets": with_ends(ranked_ids(own_keys[5], (SPANS, SPAN), VOCAB, 2), jax.random.fold_in(own_keys[5], 3), 0, VOCAB - 1).astype(jnp.int32),
        "lengths": jax.random.randint(own_keys[6], (1,), TOKENS // 4, TOKENS + 1).astype(jnp.int32),
    }


def combine_stats(first, second):
    top = jnp.maximum(first[0], second[0])
    scale_first = jnp.exp(first[0] - top)
    scale_second = jnp.exp(second[0] - top)
    total = first[1] * scale_first + second[1] * scale_second
    moment = scale_first * (first[2] + first[1] * (first[0] - top)) + scale_second * (second[2] + second[1] * (second[0] - top))
    return (top, total, moment, first[3] + second[3])

def reference(heads_out, out_weight, residual, norm_gain, head_weight, targets, lengths):
    spans, span, features = heads_out.shape
    width = out_weight.shape[1]
    count = spans * span
    hidden = jnp.dot(heads_out.reshape(count, features), out_weight, preferred_element_type=jnp.float32)
    hidden = hidden + residual.reshape(count, width).astype(jnp.float32)
    mean_square = lax.optimization_barrier(jnp.mean(hidden * hidden, axis=1, keepdims=True))
    normed = (hidden * lax.rsqrt(mean_square + 1e-05) * norm_gain.astype(jnp.float32)).astype(jnp.bfloat16)
    flat_targets = targets.reshape(count).astype(jnp.int32)
    blocks = head_weight.reshape(-1, VOC_DEV, width)
    starts = (jnp.arange(blocks.shape[0]) * VOC_DEV).astype(jnp.int32)

    def step(carry, item):
        block, start = item
        logits = lax.dot_general(normed, block, (((1,), (1,)), ((), ())), preferred_element_type=jnp.float32)
        top = lax.optimization_barrier(jnp.max(logits, axis=1))
        shifted = logits - top[:, None]
        weights = jnp.exp(shifted)
        columns = jnp.arange(VOC_DEV, dtype=jnp.int32)[None, :] + start
        chosen = lax.optimization_barrier(jnp.sum(jnp.where(columns == flat_targets[:, None], logits, jnp.float32(0.0)), axis=1))
        part = (top, lax.optimization_barrier(jnp.sum(weights, axis=1)), lax.optimization_barrier(jnp.sum(weights * shifted, axis=1)), chosen)
        return (combine_stats(carry, part), None)
    zeros = jnp.zeros((count,), jnp.float32)
    init = (jnp.full((count,), -1e+30, jnp.float32), zeros, zeros, zeros)
    stats, _ = lax.scan(step, init, (blocks, starts))
    top, total, moment, chosen = stats
    log_total = jnp.log(total)
    logprob = chosen - top - log_total
    entropy = log_total - moment / total
    live = jnp.arange(count, dtype=jnp.int32) < lengths[0]
    logprob = jnp.where(live, logprob, jnp.float32(0.0)).reshape(spans, span)
    entropy = jnp.where(live, entropy, jnp.float32(0.0)).reshape(spans, span)
    return (logprob, entropy)
```

```python
import jax
import jax.numpy as jnp
from jax import lax
from jax.experimental import pallas as pl
from jax.experimental.pallas import tpu as pltpu
from jax.sharding import PartitionSpec as P

norm_epsilon = 1e-05
MESH = pl.DeviceIdType.MESH
TENSOR, VOCAB, SEQ = 4, 2, 2
PEERS = [
    (dt, dv, ds) for dt in range(TENSOR) for dv in range(VOCAB) for ds in range(SEQ)
][1:]


def fused_kernel(
    heads_ref, weight_hbm, residual_ref, gain_ref, head_hbm, targets_ref, lengths_ref,
    logprob_ref, entropy_ref,
    weight, head, part, part_in, square_out, square_in, rows, stat_out, stat_in,
    weight_sem, head_sem, part_send, part_recv, square_send, square_recv,
    z_send, z_recv, x_send, x_recv, near_send, near_recv, far_send, far_recv,
    stat_send, stat_recv,
):
    t = lax.axis_index("tensor")
    v = lax.axis_index("vocab")
    s = lax.axis_index("seq")
    g = lax.axis_index("groups")
    depth = weight.shape[1]
    half = depth // 2
    shard = part.shape[1]
    span = TENSOR * shard
    width = VOCAB * depth

    def device(dt, dv, ds):
        return (g, lax.rem(t + dt, TENSOR), lax.rem(v + dv, VOCAB), lax.rem(s + ds, SEQ))

    def block(k):
        return lax.rem(t + TENSOR - k, TENSOR)

    def send(src, dst, send_sem, recv_sem, to):
        copy = pltpu.make_async_remote_copy(
            src_ref=src, dst_ref=dst, send_sem=send_sem, recv_sem=recv_sem,
            device_id=to, device_id_type=MESH,
        )
        copy.start()
        return copy

    weight_copy = pltpu.make_async_copy(weight_hbm, weight, weight_sem)
    weight_copy.start()
    head_copy = pltpu.make_async_copy(head_hbm, head, head_sem)
    head_copy.start()
    barrier = pltpu.get_barrier_semaphore()
    for peer in PEERS:
        pl.semaphore_signal(barrier, inc=1, device_id=device(*peer), device_id_type=MESH)

    weight_copy.wait()
    product = jnp.dot(heads_ref[0], weight[...], preferred_element_type=jnp.float32)
    part[...] = product.reshape(TENSOR, shard, depth)
    pl.semaphore_wait(barrier, len(PEERS))
    sent = []
    part_copies = [
        send(part.at[lax.rem(t + k, TENSOR)], part_in.at[k - 1],
             part_send.at[k - 1], part_recv.at[k - 1], device(k, 0, 0))
        for k in range(1, TENSOR)
    ]
    hidden = part[t] + residual_ref[0].astype(jnp.float32)
    for k in range(1, TENSOR):
        part_copies[k - 1].wait_recv()
        hidden = hidden + part_in[k - 1]
    sent += part_copies

    own_square = jnp.sum(hidden * hidden, axis=1, keepdims=True)
    square_out[...] = jnp.broadcast_to(own_square, square_out.shape)
    square_copy = send(square_out, square_in, square_send, square_recv, device(0, 1, 0))
    scaled_gain = gain_ref[...].astype(jnp.float32)
    square_copy.wait_recv()
    sent.append(square_copy)
    mean = (own_square + square_in[:, :1]) / width
    normed = hidden * lax.rsqrt(mean + norm_epsilon) * scaled_gain
    rows[0, 0, t] = jnp.concatenate([normed[:, :half], normed[:, half:]], axis=0).astype(
        jnp.bfloat16
    )

    own = rows.at[0, 0, t]
    z_copies = [
        send(own, own, z_send.at[k - 1], z_recv.at[k - 1], device(k, 0, 0))
        for k in range(1, TENSOR)
    ]
    x_copies, near_copies, far_copies = [], [], []
    for k in range(TENSOR):
        if k:
            z_copies[k - 1].wait_recv()
        here = rows.at[0, 0, block(k)]
        x_copies.append(
            send(here, rows.at[1, 0, block(k)], x_send.at[k], x_recv.at[k], device(0, 1, 0))
        )
        near_copies.append(
            send(here, rows.at[0, 1, block(k)], near_send.at[k], near_recv.at[k],
                 device(0, 0, 1))
        )
    for copy in near_copies:
        copy.wait_recv()
    head_copy.wait()

    blocks = SEQ * TENSOR
    vocab = head.shape[0]

    def partial_logits(side, column_half):
        columns = lax.rem(v + side, VOCAB) * depth + column_half * half
        tokens = rows[side].reshape(blocks * 2 * shard, half)
        out = lax.dot_general(
            tokens, head[:, pl.ds(pl.multiple_of(columns, 128), half)],
            (((1,), (1,)), ((), ())), preferred_element_type=jnp.float32,
        )
        return out.reshape(blocks, 2, shard, vocab)[:, column_half]

    logits = partial_logits(0, 0)
    for k in range(TENSOR):
        x_copies[k].wait_recv()
        far_copies.append(
            send(rows.at[1, 0, block(k)], rows.at[1, 1, block(k)], far_send.at[k],
                 far_recv.at[k], device(0, 0, 1))
        )
    logits = logits + partial_logits(0, 1)
    for copy in far_copies:
        copy.wait_recv()
    logits = logits + partial_logits(1, 0) + partial_logits(1, 1)
    logits = logits.reshape(blocks * shard, vocab)
    sent += z_copies + x_copies + near_copies + far_copies

    diagonal = lax.broadcasted_iota(jnp.int32, (span, span), 0) == lax.broadcasted_iota(
        jnp.int32, (span, span), 1
    )
    all_targets = targets_ref[...].astype(jnp.float32)
    lower, upper = all_targets[0:1], all_targets[1:2]
    own_targets = jnp.where(s == 0, lower, upper)
    other_targets = jnp.where(s == 0, upper, lower)
    target = jnp.concatenate(
        [
            jnp.sum(jnp.where(diagonal, line, 0.0), axis=1, keepdims=True)
            for line in (own_targets, other_targets)
        ],
        axis=0,
    ).astype(jnp.int32)
    start = ((t * VOCAB + v) * SEQ + s) * vocab
    columns = lax.broadcasted_iota(jnp.int32, logits.shape, 1)
    chosen = jnp.sum(
        jnp.where(columns == target - start, logits, 0.0), axis=1, keepdims=True
    )
    top = jnp.max(logits, axis=1, keepdims=True)
    shifted = logits - top
    weights = jnp.exp(shifted)
    total = jnp.sum(weights, axis=1, keepdims=True)
    moment = jnp.sum(weights * shifted, axis=1, keepdims=True)
    lane = lax.broadcasted_iota(jnp.int32, (blocks * shard, 128), 1)
    stats = jnp.where(
        lane == 0, top, jnp.where(lane == 1, total, jnp.where(lane == 2, moment, chosen))
    )
    stat_out[...] = stats.reshape(SEQ, TENSOR, shard, 128)
    stat_in[0] = stat_out[0, t]
    stat_copies = []
    for index, (dt, dv, ds) in enumerate(PEERS):
        stat_copies.append(
            send(stat_out.at[ds, lax.rem(t + dt, TENSOR)], stat_in.at[index + 1],
                 stat_send.at[index], stat_recv.at[index], device(dt, dv, ds))
        )
    for copy in stat_copies:
        copy.wait_recv()
    sent += stat_copies

    gathered = stat_in[...]
    tops = gathered[:, :, 0:1]
    top = jnp.max(tops, axis=0)
    below = tops - top[None]
    scale = jnp.exp(below)
    totals = gathered[:, :, 1:2]
    total = jnp.sum(totals * scale, axis=0)
    moment = jnp.sum(scale * (gathered[:, :, 2:3] + totals * below), axis=0)
    chosen = jnp.sum(gathered[:, :, 3:4], axis=0)
    log_total = jnp.log(total)
    logprob = chosen - top - log_total
    entropy = log_total - moment / total
    shape = (shard, shard)
    diagonal = lax.broadcasted_iota(jnp.int32, shape, 0) == lax.broadcasted_iota(
        jnp.int32, shape, 1
    )
    position = s * span + t * shard + lax.broadcasted_iota(jnp.int32, (1, shard), 1)
    live = position < lengths_ref[0]
    for ref, column in ((logprob_ref, logprob), (entropy_ref, entropy)):
        line = jnp.sum(jnp.where(diagonal, column, 0.0), axis=0, keepdims=True)
        ref[...] = jnp.where(live, line, 0.0)
    for copy in sent:
        copy.wait_send()


def fused(heads_out, out_weight, residual, norm_gain, head_weight, targets, lengths):
    shard = residual.shape[1]
    features, depth = out_weight.shape
    vocab, width = head_weight.shape
    vmem = pl.BlockSpec(memory_space=pltpu.VMEM)
    hbm = pl.BlockSpec(memory_space=pl.ANY)
    dma = pltpu.SemaphoreType.DMA
    f32, bf16 = jnp.float32, jnp.bfloat16
    hops = TENSOR - 1
    return pl.pallas_call(
        fused_kernel,
        out_shape=(jax.ShapeDtypeStruct((1, shard), f32),) * 2,
        in_specs=[vmem, hbm, vmem, vmem, hbm, vmem, pl.BlockSpec(memory_space=pltpu.SMEM)],
        out_specs=(vmem, vmem),
        scratch_shapes=[
            pltpu.VMEM((features, depth), bf16),
            pltpu.VMEM((vocab, width), bf16),
            pltpu.VMEM((TENSOR, shard, depth), f32),
            pltpu.VMEM((hops, shard, depth), f32),
            pltpu.VMEM((shard, 128), f32),
            pltpu.VMEM((shard, 128), f32),
            pltpu.VMEM((VOCAB, SEQ, TENSOR, 2 * shard, depth // 2), bf16),
            pltpu.VMEM((SEQ, TENSOR, shard, 128), f32),
            pltpu.VMEM((len(PEERS) + 1, shard, 128), f32),
            dma, dma, dma((hops,)), dma((hops,)), dma, dma,
            dma((hops,)), dma((hops,)), dma((TENSOR,)), dma((TENSOR,)),
            dma((TENSOR,)), dma((TENSOR,)), dma((TENSOR,)), dma((TENSOR,)),
            dma((len(PEERS),)), dma((len(PEERS),)),
        ],
        compiler_params=pltpu.CompilerParams(
            collective_id=0, has_side_effects=True, vmem_limit_bytes=32 * 1024 * 1024
        ),
    )(
        heads_out, out_weight, residual, norm_gain.reshape(1, depth), head_weight,
        targets, lengths,
    )


def general(heads_out, out_weight, residual, norm_gain, head_weight, targets, lengths):
    span_rows = heads_out.shape[1]
    shard_rows = residual.shape[1]
    tensor_index = lax.axis_index("tensor")
    seq_index = lax.axis_index("seq")
    tensor_count = lax.axis_size("tensor")
    seq_count = lax.axis_size("seq")
    gain = norm_gain.astype(jnp.float32)
    summed = lax.psum_scatter(
        jnp.dot(heads_out[0], out_weight, preferred_element_type=jnp.float32),
        "tensor", scatter_dimension=0, tiled=True,
    )
    hidden = summed + residual[0].astype(jnp.float32)
    squares = lax.psum(jnp.sum(hidden * hidden, axis=1), "vocab")
    width = head_weight.shape[1]
    normed = (hidden * lax.rsqrt(squares / width + norm_epsilon)[:, None] * gain).astype(
        jnp.bfloat16
    )
    full_rows = lax.all_gather(normed[None], "vocab", axis=2, tiled=True)
    logits = jnp.einsum(
        "gtd,vd->gtv",
        lax.all_gather(full_rows, ("tensor", "seq"), axis=0, tiled=True),
        head_weight,
        preferred_element_type=jnp.float32,
    )
    ordered = targets.reshape(seq_count, tensor_count, shard_rows).transpose(1, 0, 2)
    ordered = ordered.reshape(tensor_count * seq_count, shard_rows)
    own_group = tensor_index * seq_count + seq_index
    axes = ("tensor", "vocab", "seq")
    local_target = ordered - lax.axis_index(axes) * head_weight.shape[0]
    columns = lax.broadcasted_iota(jnp.int32, logits.shape, 2)
    chosen = jnp.sum(jnp.where(columns == local_target[..., None], logits, 0.0), axis=2)
    top = lax.pmax(jnp.max(logits, axis=2), axes)
    shifted = logits - top[..., None]
    weights = jnp.exp(shifted)
    total, moment, chosen = lax.psum(
        (jnp.sum(weights, axis=2), jnp.sum(weights * shifted, axis=2), chosen), axes
    )
    log_total = jnp.log(total)
    logprob = chosen - top - log_total
    entropy = log_total - moment / total
    logprob = lax.dynamic_index_in_dim(logprob, own_group, 0, keepdims=False)
    entropy = lax.dynamic_index_in_dim(entropy, own_group, 0, keepdims=False)
    positions = (
        seq_index * span_rows + tensor_index * shard_rows + jnp.arange(shard_rows, dtype=jnp.int32)
    )
    live = positions < lengths[0]
    return (jnp.where(live, logprob, 0.0)[None], jnp.where(live, entropy, 0.0)[None])


def solution(mesh):
    in_specs = (
        P(("groups", "seq"), None, "tensor"),
        P("tensor", "vocab"),
        P(("groups", "seq"), "tensor", "vocab"),
        P("vocab"),
        P(("tensor", "vocab", "seq"), None),
        P("groups", None),
        P("groups"),
    )
    out_specs = (P(("groups", "seq"), "tensor"), P(("groups", "seq"), "tensor"))
    sizes = (mesh.shape["tensor"], mesh.shape["vocab"], mesh.shape["seq"])
    body = fused if sizes == (TENSOR, VOCAB, SEQ) else general
    return jax.shard_map(
        body, mesh=mesh, in_specs=in_specs, out_specs=out_specs, check_vma=False
    )
```

```python
import jax
import jax.numpy as jnp
from jax import lax
from jax.experimental import pallas as pl
from jax.experimental.pallas import tpu as pltpu
from jax.sharding import PartitionSpec as P

norm_epsilon = 1e-05
MESH = pl.DeviceIdType.MESH
TENSOR, VOCAB, SEQ = 4, 2, 2
PEERS = [
    (dt, dv, ds) for dt in range(TENSOR) for dv in range(VOCAB) for ds in range(SEQ)
][1:]


def fused_kernel(
    heads_hbm, weight_hbm, residual_hbm, gain_ref, head_hbm, targets_hbm, lengths_hbm,
    logprob_ref, entropy_ref,
    heads_ref, residual_ref, targets_ref, lengths_ref, weight, head, part, part_in, square_out, square_in, rows, stat_out, stat_in,
    input_sem, weight_sem, head_sem, part_send, part_recv, square_send, square_recv,
    z_send, z_recv, x_send, x_recv, near_send, near_recv, far_send, far_recv,
    stat_send, stat_recv,
):
    t = lax.axis_index("tensor")
    v = lax.axis_index("vocab")
    s = lax.axis_index("seq")
    g = lax.axis_index("groups")
    depth = weight.shape[1]
    half = depth // 2
    shard = part.shape[1]
    span = TENSOR * shard
    width = VOCAB * depth

    def device(dt, dv, ds):
        return (g, lax.rem(t + dt, TENSOR), lax.rem(v + dv, VOCAB), lax.rem(s + ds, SEQ))

    def block(k):
        return lax.rem(t + TENSOR - k, TENSOR)

    def send(src, dst, send_sem, recv_sem, to):
        copy = pltpu.make_async_remote_copy(
            src_ref=src, dst_ref=dst, send_sem=send_sem, recv_sem=recv_sem,
            device_id=to, device_id_type=MESH,
        )
        copy.start()
        return copy

    heads_copy = pltpu.make_async_copy(heads_hbm, heads_ref, input_sem.at[0])
    heads_copy.start()
    weight_copy = pltpu.make_async_copy(weight_hbm, weight, weight_sem)
    weight_copy.start()
    residual_copy = pltpu.make_async_copy(residual_hbm, residual_ref, input_sem.at[1])
    residual_copy.start()
    targets_copy = pltpu.make_async_copy(targets_hbm, targets_ref, input_sem.at[2])
    targets_copy.start()
    lengths_copy = pltpu.make_async_copy(lengths_hbm, lengths_ref, input_sem.at[3])
    lengths_copy.start()
    head_copy = pltpu.make_async_copy(head_hbm, head, head_sem)
    barrier = pltpu.get_barrier_semaphore()
    for peer in PEERS:
        pl.semaphore_signal(barrier, inc=1, device_id=device(*peer), device_id_type=MESH)

    heads_copy.wait()
    weight_copy.wait()
    head_copy.start()
    product = jnp.dot(heads_ref[0], weight[...], preferred_element_type=jnp.float32)
    part[...] = product.reshape(TENSOR, shard, depth)
    pl.semaphore_wait(barrier, len(PEERS))
    sent = []
    part_copies = [
        send(part.at[lax.rem(t + k, TENSOR)], part_in.at[k - 1],
             part_send.at[k - 1], part_recv.at[k - 1], device(k, 0, 0))
        for k in range(1, TENSOR)
    ]
    residual_copy.wait()
    hidden = part[t] + residual_ref[0].astype(jnp.float32)
    for k in range(1, TENSOR):
        part_copies[k - 1].wait_recv()
        hidden = hidden + part_in[k - 1]
    sent += part_copies

    own_square = jnp.sum(hidden * hidden, axis=1, keepdims=True)
    square_out[...] = jnp.broadcast_to(own_square, square_out.shape)
    square_copy = send(square_out, square_in, square_send, square_recv, device(0, 1, 0))
    scaled_gain = gain_ref[...].astype(jnp.float32).reshape(1, depth)
    square_copy.wait_recv()
    sent.append(square_copy)
    mean = (own_square + square_in[:, :1]) / width
    normed = hidden * lax.rsqrt(mean + norm_epsilon) * scaled_gain
    rows[0, 0, t] = jnp.concatenate([normed[:, :half], normed[:, half:]], axis=0).astype(
        jnp.bfloat16
    )

    own = rows.at[0, 0, t]
    z_copies = [
        send(own, own, z_send.at[k - 1], z_recv.at[k - 1], device(k, 0, 0))
        for k in range(1, TENSOR)
    ]
    x_copies, near_copies, far_copies = [], [], []
    for k in range(TENSOR):
        if k:
            z_copies[k - 1].wait_recv()
        here = rows.at[0, 0, block(k)]
        x_copies.append(
            send(here, rows.at[1, 0, block(k)], x_send.at[k], x_recv.at[k], device(0, 1, 0))
        )
        near_copies.append(
            send(here, rows.at[0, 1, block(k)], near_send.at[k], near_recv.at[k],
                 device(0, 0, 1))
        )
    for k in range(TENSOR):
        x_copies[k].wait_recv()
        far_copies.append(
            send(rows.at[1, 0, block(k)], rows.at[1, 1, block(k)], far_send.at[k],
                 far_recv.at[k], device(0, 0, 1))
        )
    for copy in near_copies:
        copy.wait_recv()
    head_copy.wait()

    blocks = SEQ * TENSOR
    vocab = head.shape[0]

    def partial_logits(side, column_half):
        columns = lax.rem(v + side, VOCAB) * depth + column_half * half
        tokens = rows[side].reshape(blocks * 2 * shard, half)
        out = lax.dot_general(
            tokens, head[:, pl.ds(pl.multiple_of(columns, 128), half)],
            (((1,), (1,)), ((), ())), preferred_element_type=jnp.float32,
        )
        return out.reshape(blocks, 2, shard, vocab)[:, column_half]

    logits = partial_logits(0, 0)
    logits = logits + partial_logits(0, 1)
    for copy in far_copies:
        copy.wait_recv()
    logits = logits + partial_logits(1, 0) + partial_logits(1, 1)
    logits = logits.reshape(blocks * shard, vocab)
    sent += z_copies + x_copies + near_copies + far_copies

    diagonal = lax.broadcasted_iota(jnp.int32, (span, span), 0) == lax.broadcasted_iota(
        jnp.int32, (span, span), 1
    )
    targets_copy.wait()
    all_targets = targets_ref[...].astype(jnp.float32)
    lower, upper = all_targets[0:1], all_targets[1:2]
    own_targets = jnp.where(s == 0, lower, upper)
    other_targets = jnp.where(s == 0, upper, lower)
    target = jnp.concatenate(
        [
            jnp.sum(jnp.where(diagonal, line, 0.0), axis=1, keepdims=True)
            for line in (own_targets, other_targets)
        ],
        axis=0,
    ).astype(jnp.int32)
    start = ((t * VOCAB + v) * SEQ + s) * vocab
    columns = lax.broadcasted_iota(jnp.int32, logits.shape, 1)
    chosen = jnp.sum(
        jnp.where(columns == target - start, logits, 0.0), axis=1, keepdims=True
    )
    top = jnp.max(logits, axis=1, keepdims=True)
    shifted = logits - top
    weights = jnp.exp(shifted)
    total = jnp.sum(weights, axis=1, keepdims=True)
    moment = jnp.sum(weights * shifted, axis=1, keepdims=True)
    lane = lax.broadcasted_iota(jnp.int32, (blocks * shard, 128), 1)
    stats = jnp.where(
        lane == 0, top, jnp.where(lane == 1, total, jnp.where(lane == 2, moment, chosen))
    )
    stat_out[...] = stats.reshape(SEQ, TENSOR, shard, 128)
    stat_in[0] = stat_out[0, t]
    stat_copies = []
    for index, (dt, dv, ds) in enumerate(PEERS):
        stat_copies.append(
            send(stat_out.at[ds, lax.rem(t + dt, TENSOR)], stat_in.at[index + 1],
                 stat_send.at[index], stat_recv.at[index], device(dt, dv, ds))
        )
    for copy in stat_copies:
        copy.wait_recv()
    sent += stat_copies

    gathered = stat_in[...]
    tops = gathered[:, :, 0:1]
    top = jnp.max(tops, axis=0)
    below = tops - top[None]
    scale = jnp.exp(below)
    totals = gathered[:, :, 1:2]
    total = jnp.sum(totals * scale, axis=0)
    moment = jnp.sum(scale * (gathered[:, :, 2:3] + totals * below), axis=0)
    chosen = jnp.sum(gathered[:, :, 3:4], axis=0)
    log_total = jnp.log(total)
    logprob = chosen - top - log_total
    entropy = log_total - moment / total
    shape = (shard, shard)
    diagonal = lax.broadcasted_iota(jnp.int32, shape, 0) == lax.broadcasted_iota(
        jnp.int32, shape, 1
    )
    lengths_copy.wait()
    position = s * span + t * shard + lax.broadcasted_iota(jnp.int32, (1, shard), 1)
    live = position < lengths_ref[0]
    for ref, column in ((logprob_ref, logprob), (entropy_ref, entropy)):
        line = jnp.sum(jnp.where(diagonal, column, 0.0), axis=0, keepdims=True)
        ref[...] = jnp.where(live, line, 0.0)
    for copy in sent:
        copy.wait_send()


def fused(heads_out, out_weight, residual, norm_gain, head_weight, targets, lengths):
    shard = residual.shape[1]
    features, depth = out_weight.shape
    vocab, width = head_weight.shape
    vmem = pl.BlockSpec(memory_space=pltpu.VMEM)
    hbm = pl.BlockSpec(memory_space=pl.ANY)
    dma = pltpu.SemaphoreType.DMA
    f32, bf16 = jnp.float32, jnp.bfloat16
    hops = TENSOR - 1
    return pl.pallas_call(
        fused_kernel,
        out_shape=(jax.ShapeDtypeStruct((1, shard), f32),) * 2,
        in_specs=[hbm, hbm, hbm, vmem, hbm, hbm, hbm],
        out_specs=(vmem, vmem),
        scratch_shapes=[
            pltpu.VMEM(heads_out.shape, bf16),
            pltpu.VMEM(residual.shape, bf16),
            pltpu.VMEM(targets.shape, jnp.int32),
            pltpu.SMEM(lengths.shape, jnp.int32),
            pltpu.VMEM((features, depth), bf16),
            pltpu.VMEM((vocab, width), bf16),
            pltpu.VMEM((TENSOR, shard, depth), f32),
            pltpu.VMEM((hops, shard, depth), f32),
            pltpu.VMEM((shard, 128), f32),
            pltpu.VMEM((shard, 128), f32),
            pltpu.VMEM((VOCAB, SEQ, TENSOR, 2 * shard, depth // 2), bf16),
            pltpu.VMEM((SEQ, TENSOR, shard, 128), f32),
            pltpu.VMEM((len(PEERS) + 1, shard, 128), f32),
            dma((4,)), dma, dma, dma((hops,)), dma((hops,)), dma, dma,
            dma((hops,)), dma((hops,)), dma((TENSOR,)), dma((TENSOR,)),
            dma((TENSOR,)), dma((TENSOR,)), dma((TENSOR,)), dma((TENSOR,)),
            dma((len(PEERS),)), dma((len(PEERS),)),
        ],
        compiler_params=pltpu.CompilerParams(
            collective_id=0, has_side_effects=True, vmem_limit_bytes=60 * 1024 * 1024
        ),
    )(
        heads_out, out_weight, residual, norm_gain, head_weight,
        targets, lengths,
    )


def general(heads_out, out_weight, residual, norm_gain, head_weight, targets, lengths):
    span_rows = heads_out.shape[1]
    shard_rows = residual.shape[1]
    tensor_index = lax.axis_index("tensor")
    seq_index = lax.axis_index("seq")
    tensor_count = lax.axis_size("tensor")
    seq_count = lax.axis_size("seq")
    gain = norm_gain.astype(jnp.float32)
    summed = lax.psum_scatter(
        jnp.dot(heads_out[0], out_weight, preferred_element_type=jnp.float32),
        "tensor", scatter_dimension=0, tiled=True,
    )
    hidden = summed + residual[0].astype(jnp.float32)
    squares = lax.psum(jnp.sum(hidden * hidden, axis=1), "vocab")
    width = head_weight.shape[1]
    normed = (hidden * lax.rsqrt(squares / width + norm_epsilon)[:, None] * gain).astype(
        jnp.bfloat16
    )
    full_rows = lax.all_gather(normed[None], "vocab", axis=2, tiled=True)
    logits = jnp.einsum(
        "gtd,vd->gtv",
        lax.all_gather(full_rows, ("tensor", "seq"), axis=0, tiled=True),
        head_weight,
        preferred_element_type=jnp.float32,
    )
    ordered = targets.reshape(seq_count, tensor_count, shard_rows).transpose(1, 0, 2)
    ordered = ordered.reshape(tensor_count * seq_count, shard_rows)
    own_group = tensor_index * seq_count + seq_index
    axes = ("tensor", "vocab", "seq")
    local_target = ordered - lax.axis_index(axes) * head_weight.shape[0]
    columns = lax.broadcasted_iota(jnp.int32, logits.shape, 2)
    chosen = jnp.sum(jnp.where(columns == local_target[..., None], logits, 0.0), axis=2)
    top = lax.pmax(jnp.max(logits, axis=2), axes)
    shifted = logits - top[..., None]
    weights = jnp.exp(shifted)
    total, moment, chosen = lax.psum(
        (jnp.sum(weights, axis=2), jnp.sum(weights * shifted, axis=2), chosen), axes
    )
    log_total = jnp.log(total)
    logprob = chosen - top - log_total
    entropy = log_total - moment / total
    logprob = lax.dynamic_index_in_dim(logprob, own_group, 0, keepdims=False)
    entropy = lax.dynamic_index_in_dim(entropy, own_group, 0, keepdims=False)
    positions = (
        seq_index * span_rows + tensor_index * shard_rows + jnp.arange(shard_rows, dtype=jnp.int32)
    )
    live = positions < lengths[0]
    return (jnp.where(live, logprob, 0.0)[None], jnp.where(live, entropy, 0.0)[None])


def solution(mesh):
    in_specs = (
        P(("groups", "seq"), None, "tensor"),
        P("tensor", "vocab"),
        P(("groups", "seq"), "tensor", "vocab"),
        P("vocab"),
        P(("tensor", "vocab", "seq"), None),
        P("groups", None),
        P("groups"),
    )
    out_specs = (P(("groups", "seq"), "tensor"), P(("groups", "seq"), "tensor"))
    sizes = (mesh.shape["tensor"], mesh.shape["vocab"], mesh.shape["seq"])
    body = fused if sizes == (TENSOR, VOCAB, SEQ) else general
    return jax.shard_map(
        body, mesh=mesh, in_specs=in_specs, out_specs=out_specs, check_vma=False
    )
```

```python
import jax
import jax.numpy as jnp
from jax import lax
from jax.experimental import pallas as pl
from jax.experimental.pallas import tpu as pltpu
from jax.sharding import PartitionSpec as P

norm_epsilon = 1e-05
MESH = pl.DeviceIdType.MESH
TENSOR, VOCAB, SEQ = 4, 2, 2
PEERS = [
    (dt, dv, ds) for dt in range(TENSOR) for dv in range(VOCAB) for ds in range(SEQ)
][1:]


def fused_kernel(
    heads_hbm, weight_hbm, residual_hbm, gain_ref, head_hbm, targets_hbm, lengths_hbm,
    out_ref,
    heads_ref, residual_ref, targets_ref, lengths_ref, weight, head, part, part_in, square_out, square_in, rows, stat_out, stat_in,
    input_sem, weight_sem, head_sem, part_send, part_recv, square_send, square_recv,
    z_send, z_recv, x_send, x_recv, near_send, near_recv, far_send, far_recv,
    stat_send, stat_recv,
):
    t = lax.axis_index("tensor")
    v = lax.axis_index("vocab")
    s = lax.axis_index("seq")
    g = lax.axis_index("groups")
    depth = weight.shape[1]
    half = depth // 2
    shard = part.shape[1]
    span = TENSOR * shard
    width = VOCAB * depth

    def device(dt, dv, ds):
        return (g, lax.rem(t + dt, TENSOR), lax.rem(v + dv, VOCAB), lax.rem(s + ds, SEQ))

    def block(k):
        return lax.rem(t + TENSOR - k, TENSOR)

    def send(src, dst, send_sem, recv_sem, to):
        copy = pltpu.make_async_remote_copy(
            src_ref=src, dst_ref=dst, send_sem=send_sem, recv_sem=recv_sem,
            device_id=to, device_id_type=MESH,
        )
        copy.start()
        return copy

    heads_copy = pltpu.make_async_copy(heads_hbm, heads_ref, input_sem.at[0])
    heads_copy.start()
    weight_copy = pltpu.make_async_copy(weight_hbm, weight, weight_sem)
    weight_copy.start()
    residual_copy = pltpu.make_async_copy(residual_hbm, residual_ref, input_sem.at[1])
    residual_copy.start()
    targets_copy = pltpu.make_async_copy(targets_hbm, targets_ref, input_sem.at[2])
    targets_copy.start()
    lengths_copy = pltpu.make_async_copy(lengths_hbm, lengths_ref, input_sem.at[3])
    lengths_copy.start()
    head_copy = pltpu.make_async_copy(head_hbm, head, head_sem)
    barrier = pltpu.get_barrier_semaphore()
    for peer in PEERS:
        pl.semaphore_signal(barrier, inc=1, device_id=device(*peer), device_id_type=MESH)

    heads_copy.wait()
    weight_copy.wait()
    head_copy.start()
    product = jnp.dot(heads_ref[0], weight[...], preferred_element_type=jnp.float32)
    part[...] = product.reshape(TENSOR, shard, depth)
    pl.semaphore_wait(barrier, len(PEERS))
    sent = []
    part_copies = [
        send(part.at[lax.rem(t + k, TENSOR)], part_in.at[k - 1],
             part_send.at[k - 1], part_recv.at[k - 1], device(k, 0, 0))
        for k in range(1, TENSOR)
    ]
    residual_copy.wait()
    hidden = part[t] + residual_ref[0].astype(jnp.float32)
    for k in range(1, TENSOR):
        part_copies[k - 1].wait_recv()
        hidden = hidden + part_in[k - 1]
    sent += part_copies

    own_square = jnp.sum(hidden * hidden, axis=1, keepdims=True)
    square_out[...] = jnp.broadcast_to(own_square, square_out.shape)
    square_copy = send(square_out, square_in, square_send, square_recv, device(0, 1, 0))
    scaled_gain = gain_ref[...].astype(jnp.float32).reshape(1, depth)
    square_copy.wait_recv()
    sent.append(square_copy)
    mean = (own_square + square_in[:, :1]) / width
    normed = hidden * lax.rsqrt(mean + norm_epsilon) * scaled_gain
    rows[0, 0, t] = jnp.concatenate([normed[:, :half], normed[:, half:]], axis=0).astype(
        jnp.bfloat16
    )

    own = rows.at[0, 0, t]
    z_copies = [
        send(own, own, z_send.at[k - 1], z_recv.at[k - 1], device(k, 0, 0))
        for k in range(1, TENSOR)
    ]
    x_copies = []
    for k in range(TENSOR):
        if k:
            z_copies[k - 1].wait_recv()
        here = rows.at[0, 0, block(k)]
        x_copies.append(
            send(here, rows.at[1, 0, block(k)], x_send.at[k], x_recv.at[k], device(0, 1, 0))
        )
    near_copies = [send(rows.at[0, 0], rows.at[0, 1], near_send, near_recv, device(0, 0, 1))]
    for k in range(TENSOR):
        x_copies[k].wait_recv()
    far_copies = [send(rows.at[1, 0], rows.at[1, 1], far_send, far_recv, device(0, 0, 1))]
    for copy in near_copies:
        copy.wait_recv()
    head_copy.wait()

    blocks = SEQ * TENSOR
    vocab = head.shape[0]

    def partial_logits(side, column_half):
        columns = lax.rem(v + side, VOCAB) * depth + column_half * half
        tokens = rows[side].reshape(blocks * 2 * shard, half)
        out = lax.dot_general(
            tokens, head[:, pl.ds(pl.multiple_of(columns, 128), half)],
            (((1,), (1,)), ((), ())), preferred_element_type=jnp.float32,
        )
        return out.reshape(blocks, 2, shard, vocab)[:, column_half]

    logits = partial_logits(0, 0)
    logits = logits + partial_logits(0, 1)
    for copy in far_copies:
        copy.wait_recv()
    logits = logits + partial_logits(1, 0) + partial_logits(1, 1)
    logits = logits.reshape(blocks * shard, vocab)
    sent += z_copies + x_copies + near_copies + far_copies

    diagonal = lax.broadcasted_iota(jnp.int32, (span, span), 0) == lax.broadcasted_iota(
        jnp.int32, (span, span), 1
    )
    targets_copy.wait()
    all_targets = targets_ref[...].astype(jnp.float32)
    lower, upper = all_targets[0:1], all_targets[1:2]
    own_targets = jnp.where(s == 0, lower, upper)
    other_targets = jnp.where(s == 0, upper, lower)
    target = jnp.concatenate(
        [
            jnp.sum(jnp.where(diagonal, line, 0.0), axis=1, keepdims=True)
            for line in (own_targets, other_targets)
        ],
        axis=0,
    ).astype(jnp.int32)
    start = ((t * VOCAB + v) * SEQ + s) * vocab
    columns = lax.broadcasted_iota(jnp.int32, logits.shape, 1)
    chosen = jnp.sum(
        jnp.where(columns == target - start, logits, 0.0), axis=1, keepdims=True
    )
    top = jnp.max(logits, axis=1, keepdims=True)
    shifted = logits - top
    weights = jnp.exp(shifted)
    total = jnp.sum(weights, axis=1, keepdims=True)
    moment = jnp.sum(weights * shifted, axis=1, keepdims=True)
    lane = lax.broadcasted_iota(jnp.int32, (blocks * shard, 128), 1)
    stats = jnp.where(
        lane == 0, top, jnp.where(lane == 1, total, jnp.where(lane == 2, moment, chosen))
    )
    stat_out[...] = stats.reshape(SEQ, TENSOR, shard, 128)
    stat_in[0] = stat_out[0, t]
    stat_copies = []
    for index, (dt, dv, ds) in enumerate(PEERS):
        stat_copies.append(
            send(stat_out.at[ds, lax.rem(t + dt, TENSOR)], stat_in.at[index + 1],
                 stat_send.at[index], stat_recv.at[index], device(dt, dv, ds))
        )
    for copy in stat_copies:
        copy.wait_recv()
    sent += stat_copies

    gathered = stat_in[...]
    tops = gathered[:, :, 0:1]
    top = jnp.max(tops, axis=0)
    below = tops - top[None]
    scale = jnp.exp(below)
    totals = gathered[:, :, 1:2]
    total = jnp.sum(totals * scale, axis=0)
    moment = jnp.sum(scale * (gathered[:, :, 2:3] + totals * below), axis=0)
    chosen = jnp.sum(gathered[:, :, 3:4], axis=0)
    log_total = jnp.log(total)
    logprob = chosen - top - log_total
    entropy = log_total - moment / total
    shape = (shard, shard)
    diagonal = lax.broadcasted_iota(jnp.int32, shape, 0) == lax.broadcasted_iota(
        jnp.int32, shape, 1
    )
    lengths_copy.wait()
    position = s * span + t * shard + lax.broadcasted_iota(jnp.int32, (1, shard), 1)
    live = position < lengths_ref[0]
    for index, column in enumerate((logprob, entropy)):
        line = jnp.sum(jnp.where(diagonal, column, 0.0), axis=0, keepdims=True)
        out_ref[index] = jnp.where(live, line, 0.0)
    for copy in sent:
        copy.wait_send()


def fused(heads_out, out_weight, residual, norm_gain, head_weight, targets, lengths):
    shard = residual.shape[1]
    features, depth = out_weight.shape
    vocab, width = head_weight.shape
    vmem = pl.BlockSpec(memory_space=pltpu.VMEM)
    hbm = pl.BlockSpec(memory_space=pl.ANY)
    dma = pltpu.SemaphoreType.DMA
    f32, bf16 = jnp.float32, jnp.bfloat16
    hops = TENSOR - 1
    both = pl.pallas_call(
        fused_kernel,
        out_shape=jax.ShapeDtypeStruct((2, 1, shard), f32),
        in_specs=[hbm, hbm, hbm, vmem, hbm, hbm, hbm],
        out_specs=vmem,
        scratch_shapes=[
            pltpu.VMEM(heads_out.shape, bf16),
            pltpu.VMEM(residual.shape, bf16),
            pltpu.VMEM(targets.shape, jnp.int32),
            pltpu.SMEM(lengths.shape, jnp.int32),
            pltpu.VMEM((features, depth), bf16),
            pltpu.VMEM((vocab, width), bf16),
            pltpu.VMEM((TENSOR, shard, depth), f32),
            pltpu.VMEM((hops, shard, depth), f32),
            pltpu.VMEM((shard, 128), f32),
            pltpu.VMEM((shard, 128), f32),
            pltpu.VMEM((VOCAB, SEQ, TENSOR, 2 * shard, depth // 2), bf16),
            pltpu.VMEM((SEQ, TENSOR, shard, 128), f32),
            pltpu.VMEM((len(PEERS) + 1, shard, 128), f32),
            dma((4,)), dma, dma, dma((hops,)), dma((hops,)), dma, dma,
            dma((hops,)), dma((hops,)), dma((TENSOR,)), dma((TENSOR,)),
            dma, dma, dma, dma,
            dma((len(PEERS),)), dma((len(PEERS),)),
        ],
        compiler_params=pltpu.CompilerParams(
            collective_id=0, has_side_effects=True, vmem_limit_bytes=60 * 1024 * 1024
        ),
    )(
        heads_out, out_weight, residual, norm_gain, head_weight,
        targets, lengths,
    )
    return (both[0], both[1])


def general(heads_out, out_weight, residual, norm_gain, head_weight, targets, lengths):
    span_rows = heads_out.shape[1]
    shard_rows = residual.shape[1]
    tensor_index = lax.axis_index("tensor")
    seq_index = lax.axis_index("seq")
    tensor_count = lax.axis_size("tensor")
    seq_count = lax.axis_size("seq")
    gain = norm_gain.astype(jnp.float32)
    summed = lax.psum_scatter(
        jnp.dot(heads_out[0], out_weight, preferred_element_type=jnp.float32),
        "tensor", scatter_dimension=0, tiled=True,
    )
    hidden = summed + residual[0].astype(jnp.float32)
    squares = lax.psum(jnp.sum(hidden * hidden, axis=1), "vocab")
    width = head_weight.shape[1]
    normed = (hidden * lax.rsqrt(squares / width + norm_epsilon)[:, None] * gain).astype(
        jnp.bfloat16
    )
    full_rows = lax.all_gather(normed[None], "vocab", axis=2, tiled=True)
    logits = jnp.einsum(
        "gtd,vd->gtv",
        lax.all_gather(full_rows, ("tensor", "seq"), axis=0, tiled=True),
        head_weight,
        preferred_element_type=jnp.float32,
    )
    ordered = targets.reshape(seq_count, tensor_count, shard_rows).transpose(1, 0, 2)
    ordered = ordered.reshape(tensor_count * seq_count, shard_rows)
    own_group = tensor_index * seq_count + seq_index
    axes = ("tensor", "vocab", "seq")
    local_target = ordered - lax.axis_index(axes) * head_weight.shape[0]
    columns = lax.broadcasted_iota(jnp.int32, logits.shape, 2)
    chosen = jnp.sum(jnp.where(columns == local_target[..., None], logits, 0.0), axis=2)
    top = lax.pmax(jnp.max(logits, axis=2), axes)
    shifted = logits - top[..., None]
    weights = jnp.exp(shifted)
    total, moment, chosen = lax.psum(
        (jnp.sum(weights, axis=2), jnp.sum(weights * shifted, axis=2), chosen), axes
    )
    log_total = jnp.log(total)
    logprob = chosen - top - log_total
    entropy = log_total - moment / total
    logprob = lax.dynamic_index_in_dim(logprob, own_group, 0, keepdims=False)
    entropy = lax.dynamic_index_in_dim(entropy, own_group, 0, keepdims=False)
    positions = (
        seq_index * span_rows + tensor_index * shard_rows + jnp.arange(shard_rows, dtype=jnp.int32)
    )
    live = positions < lengths[0]
    return (jnp.where(live, logprob, 0.0)[None], jnp.where(live, entropy, 0.0)[None])


def solution(mesh):
    in_specs = (
        P(("groups", "seq"), None, "tensor"),
        P("tensor", "vocab"),
        P(("groups", "seq"), "tensor", "vocab"),
        P("vocab"),
        P(("tensor", "vocab", "seq"), None),
        P("groups", None),
        P("groups"),
    )
    out_specs = (P(("groups", "seq"), "tensor"), P(("groups", "seq"), "tensor"))
    sizes = (mesh.shape["tensor"], mesh.shape["vocab"], mesh.shape["seq"])
    body = fused if sizes == (TENSOR, VOCAB, SEQ) else general
    return jax.shard_map(
        body, mesh=mesh, in_specs=in_specs, out_specs=out_specs, check_vma=False
    )
```

```python
import jax
import jax.numpy as jnp
from jax import lax
from jax.experimental import pallas as pl
from jax.experimental.pallas import tpu as pltpu
from jax.sharding import PartitionSpec as P

norm_epsilon = 1e-05
MESH = pl.DeviceIdType.MESH
TENSOR, VOCAB, SEQ = 4, 2, 2
PEERS = [
    (dt, dv, ds) for dt in range(TENSOR) for dv in range(VOCAB) for ds in range(SEQ)
][1:]


def fused_kernel(
    heads_hbm, weight_hbm, residual_hbm, gain_hbm, head_hbm, targets_hbm, lengths_hbm,
    out_ref,
    heads_ref, residual_ref, gain_ref, targets_ref, lengths_ref, weight, head, part, part_in, square_out, square_in, rows, stat_out, stat_in,
    input_sem, weight_sem, head_sem, part_send, part_recv, square_send, square_recv,
    z_send, z_recv, x_send, x_recv, near_send, near_recv, far_send, far_recv,
    stat_send, stat_recv,
):
    t = lax.axis_index("tensor")
    v = lax.axis_index("vocab")
    s = lax.axis_index("seq")
    g = lax.axis_index("groups")
    depth = weight.shape[1]
    half = depth // 2
    shard = part.shape[1]
    span = TENSOR * shard
    width = VOCAB * depth

    def device(dt, dv, ds):
        return (g, lax.rem(t + dt, TENSOR), lax.rem(v + dv, VOCAB), lax.rem(s + ds, SEQ))

    def block(k):
        return lax.rem(t + TENSOR - k, TENSOR)

    def send(src, dst, send_sem, recv_sem, to):
        copy = pltpu.make_async_remote_copy(
            src_ref=src, dst_ref=dst, send_sem=send_sem, recv_sem=recv_sem,
            device_id=to, device_id_type=MESH,
        )
        copy.start()
        return copy

    barrier = pltpu.get_barrier_semaphore()
    for peer in PEERS:
        pl.semaphore_signal(barrier, inc=1, device_id=device(*peer), device_id_type=MESH)
    heads_copy = pltpu.make_async_copy(heads_hbm, heads_ref, input_sem.at[0])
    heads_copy.start()
    weight_copy = pltpu.make_async_copy(weight_hbm, weight, weight_sem)
    weight_copy.start()
    residual_copy = pltpu.make_async_copy(residual_hbm, residual_ref, input_sem.at[1])
    residual_copy.start()
    gain_copy = pltpu.make_async_copy(gain_hbm, gain_ref, input_sem.at[4])
    gain_copy.start()
    targets_copy = pltpu.make_async_copy(targets_hbm, targets_ref, input_sem.at[2])
    targets_copy.start()
    lengths_copy = pltpu.make_async_copy(lengths_hbm, lengths_ref, input_sem.at[3])
    lengths_copy.start()
    head_copy = pltpu.make_async_copy(head_hbm, head, head_sem)

    heads_copy.wait()
    weight_copy.wait()
    head_copy.start()
    product = jnp.dot(heads_ref[0], weight[...], preferred_element_type=jnp.float32)
    part[...] = product.reshape(TENSOR, shard, depth)
    pl.semaphore_wait(barrier, len(PEERS))
    sent = []
    part_copies = [
        send(part.at[lax.rem(t + k, TENSOR)], part_in.at[k - 1],
             part_send.at[k - 1], part_recv.at[k - 1], device(k, 0, 0))
        for k in range(1, TENSOR)
    ]
    residual_copy.wait()
    hidden = part[t] + residual_ref[0].astype(jnp.float32)
    for k in range(1, TENSOR):
        part_copies[k - 1].wait_recv()
        hidden = hidden + part_in[k - 1]
    sent += part_copies

    own_square = jnp.sum(hidden * hidden, axis=1, keepdims=True)
    square_out[...] = jnp.broadcast_to(own_square, square_out.shape)
    square_copy = send(square_out, square_in, square_send, square_recv, device(0, 1, 0))
    gain_copy.wait()
    scaled_gain = gain_ref[...].astype(jnp.float32).reshape(1, depth)
    square_copy.wait_recv()
    sent.append(square_copy)
    mean = (own_square + square_in[:, :1]) / width
    normed = hidden * lax.rsqrt(mean + norm_epsilon) * scaled_gain
    rows[0, 0, t] = jnp.concatenate([normed[:, :half], normed[:, half:]], axis=0).astype(
        jnp.bfloat16
    )

    own = rows.at[0, 0, t]
    z_copies = [
        send(own, own, z_send.at[k - 1], z_recv.at[k - 1], device(k, 0, 0))
        for k in range(1, TENSOR)
    ]
    x_copies = []
    for k in range(TENSOR):
        if k:
            z_copies[k - 1].wait_recv()
        here = rows.at[0, 0, block(k)]
        x_copies.append(
            send(here, rows.at[1, 0, block(k)], x_send.at[k], x_recv.at[k], device(0, 1, 0))
        )
    near_copies = [send(rows.at[0, 0], rows.at[0, 1], near_send, near_recv, device(0, 0, 1))]
    for k in range(TENSOR):
        x_copies[k].wait_recv()
    far_copies = [send(rows.at[1, 0], rows.at[1, 1], far_send, far_recv, device(0, 0, 1))]
    for copy in near_copies:
        copy.wait_recv()
    head_copy.wait()

    blocks = SEQ * TENSOR
    vocab = head.shape[0]

    def partial_logits(side, column_half):
        columns = lax.rem(v + side, VOCAB) * depth + column_half * half
        tokens = rows[side].reshape(blocks * 2 * shard, half)
        out = lax.dot_general(
            tokens, head[:, pl.ds(pl.multiple_of(columns, 128), half)],
            (((1,), (1,)), ((), ())), preferred_element_type=jnp.float32,
        )
        return out.reshape(blocks, 2, shard, vocab)[:, column_half]

    logits = partial_logits(0, 0)
    logits = logits + partial_logits(0, 1)
    for copy in far_copies:
        copy.wait_recv()
    logits = logits + partial_logits(1, 0) + partial_logits(1, 1)
    logits = logits.reshape(blocks * shard, vocab)
    sent += z_copies + x_copies + near_copies + far_copies

    diagonal = lax.broadcasted_iota(jnp.int32, (span, span), 0) == lax.broadcasted_iota(
        jnp.int32, (span, span), 1
    )
    targets_copy.wait()
    all_targets = targets_ref[...].astype(jnp.float32)
    lower, upper = all_targets[0:1], all_targets[1:2]
    own_targets = jnp.where(s == 0, lower, upper)
    other_targets = jnp.where(s == 0, upper, lower)
    target = jnp.concatenate(
        [
            jnp.sum(jnp.where(diagonal, line, 0.0), axis=1, keepdims=True)
            for line in (own_targets, other_targets)
        ],
        axis=0,
    ).astype(jnp.int32)
    start = ((t * VOCAB + v) * SEQ + s) * vocab
    columns = lax.broadcasted_iota(jnp.int32, logits.shape, 1)
    chosen = jnp.sum(
        jnp.where(columns == target - start, logits, 0.0), axis=1, keepdims=True
    )
    top = jnp.max(logits, axis=1, keepdims=True)
    shifted = logits - top
    weights = jnp.exp(shifted)
    total = jnp.sum(weights, axis=1, keepdims=True)
    moment = jnp.sum(weights * shifted, axis=1, keepdims=True)
    lane = lax.broadcasted_iota(jnp.int32, (blocks * shard, 128), 1)
    stats = jnp.where(
        lane == 0, top, jnp.where(lane == 1, total, jnp.where(lane == 2, moment, chosen))
    )
    stat_out[...] = stats.reshape(SEQ, TENSOR, shard, 128)
    stat_in[0] = stat_out[0, t]
    stat_copies = []
    for index, (dt, dv, ds) in enumerate(PEERS):
        stat_copies.append(
            send(stat_out.at[ds, lax.rem(t + dt, TENSOR)], stat_in.at[index + 1],
                 stat_send.at[index], stat_recv.at[index], device(dt, dv, ds))
        )
    for copy in stat_copies:
        copy.wait_recv()
    sent += stat_copies

    gathered = stat_in[...]
    tops = gathered[:, :, 0:1]
    top = jnp.max(tops, axis=0)
    below = tops - top[None]
    scale = jnp.exp(below)
    totals = gathered[:, :, 1:2]
    total = jnp.sum(totals * scale, axis=0)
    moment = jnp.sum(scale * (gathered[:, :, 2:3] + totals * below), axis=0)
    chosen = jnp.sum(gathered[:, :, 3:4], axis=0)
    log_total = jnp.log(total)
    logprob = chosen - top - log_total
    entropy = log_total - moment / total
    shape = (shard, shard)
    diagonal = lax.broadcasted_iota(jnp.int32, shape, 0) == lax.broadcasted_iota(
        jnp.int32, shape, 1
    )
    lengths_copy.wait()
    position = s * span + t * shard + lax.broadcasted_iota(jnp.int32, (1, shard), 1)
    live = position < lengths_ref[0]
    for index, column in enumerate((logprob, entropy)):
        line = jnp.sum(jnp.where(diagonal, column, 0.0), axis=0, keepdims=True)
        out_ref[index] = jnp.where(live, line, 0.0)
    for copy in sent:
        copy.wait_send()


def fused(heads_out, out_weight, residual, norm_gain, head_weight, targets, lengths):
    shard = residual.shape[1]
    features, depth = out_weight.shape
    vocab, width = head_weight.shape
    vmem = pl.BlockSpec(memory_space=pltpu.VMEM)
    hbm = pl.BlockSpec(memory_space=pl.ANY)
    dma = pltpu.SemaphoreType.DMA
    f32, bf16 = jnp.float32, jnp.bfloat16
    hops = TENSOR - 1
    both = pl.pallas_call(
        fused_kernel,
        out_shape=jax.ShapeDtypeStruct((2, 1, shard), f32),
        in_specs=[hbm] * 7,
        out_specs=vmem,
        scratch_shapes=[
            pltpu.VMEM(heads_out.shape, bf16),
            pltpu.VMEM(residual.shape, bf16),
            pltpu.VMEM(norm_gain.shape, bf16),
            pltpu.VMEM(targets.shape, jnp.int32),
            pltpu.SMEM(lengths.shape, jnp.int32),
            pltpu.VMEM((features, depth), bf16),
            pltpu.VMEM((vocab, width), bf16),
            pltpu.VMEM((TENSOR, shard, depth), f32),
            pltpu.VMEM((hops, shard, depth), f32),
            pltpu.VMEM((shard, 128), f32),
            pltpu.VMEM((shard, 128), f32),
            pltpu.VMEM((VOCAB, SEQ, TENSOR, 2 * shard, depth // 2), bf16),
            pltpu.VMEM((SEQ, TENSOR, shard, 128), f32),
            pltpu.VMEM((len(PEERS) + 1, shard, 128), f32),
            dma((5,)), dma, dma, dma((hops,)), dma((hops,)), dma, dma,
            dma((hops,)), dma((hops,)), dma((TENSOR,)), dma((TENSOR,)),
            dma, dma, dma, dma,
            dma((len(PEERS),)), dma((len(PEERS),)),
        ],
        compiler_params=pltpu.CompilerParams(
            collective_id=0, has_side_effects=True, vmem_limit_bytes=60 * 1024 * 1024
        ),
    )(
        heads_out, out_weight, residual, norm_gain, head_weight,
        targets, lengths,
    )
    return (both[0], both[1])


def general(heads_out, out_weight, residual, norm_gain, head_weight, targets, lengths):
    span_rows = heads_out.shape[1]
    shard_rows = residual.shape[1]
    tensor_index = lax.axis_index("tensor")
    seq_index = lax.axis_index("seq")
    tensor_count = lax.axis_size("tensor")
    seq_count = lax.axis_size("seq")
    gain = norm_gain.astype(jnp.float32)
    summed = lax.psum_scatter(
        jnp.dot(heads_out[0], out_weight, preferred_element_type=jnp.float32),
        "tensor", scatter_dimension=0, tiled=True,
    )
    hidden = summed + residual[0].astype(jnp.float32)
    squares = lax.psum(jnp.sum(hidden * hidden, axis=1), "vocab")
    width = head_weight.shape[1]
    normed = (hidden * lax.rsqrt(squares / width + norm_epsilon)[:, None] * gain).astype(
        jnp.bfloat16
    )
    full_rows = lax.all_gather(normed[None], "vocab", axis=2, tiled=True)
    logits = jnp.einsum(
        "gtd,vd->gtv",
        lax.all_gather(full_rows, ("tensor", "seq"), axis=0, tiled=True),
        head_weight,
        preferred_element_type=jnp.float32,
    )
    ordered = targets.reshape(seq_count, tensor_count, shard_rows).transpose(1, 0, 2)
    ordered = ordered.reshape(tensor_count * seq_count, shard_rows)
    own_group = tensor_index * seq_count + seq_index
    axes = ("tensor", "vocab", "seq")
    local_target = ordered - lax.axis_index(axes) * head_weight.shape[0]
    columns = lax.broadcasted_iota(jnp.int32, logits.shape, 2)
    chosen = jnp.sum(jnp.where(columns == local_target[..., None], logits, 0.0), axis=2)
    top = lax.pmax(jnp.max(logits, axis=2), axes)
    shifted = logits - top[..., None]
    weights = jnp.exp(shifted)
    total, moment, chosen = lax.psum(
        (jnp.sum(weights, axis=2), jnp.sum(weights * shifted, axis=2), chosen), axes
    )
    log_total = jnp.log(total)
    logprob = chosen - top - log_total
    entropy = log_total - moment / total
    logprob = lax.dynamic_index_in_dim(logprob, own_group, 0, keepdims=False)
    entropy = lax.dynamic_index_in_dim(entropy, own_group, 0, keepdims=False)
    positions = (
        seq_index * span_rows + tensor_index * shard_rows + jnp.arange(shard_rows, dtype=jnp.int32)
    )
    live = positions < lengths[0]
    return (jnp.where(live, logprob, 0.0)[None], jnp.where(live, entropy, 0.0)[None])


def solution(mesh):
    in_specs = (
        P(("groups", "seq"), None, "tensor"),
        P("tensor", "vocab"),
        P(("groups", "seq"), "tensor", "vocab"),
        P("vocab"),
        P(("tensor", "vocab", "seq"), None),
        P("groups", None),
        P("groups"),
    )
    out_specs = (P(("groups", "seq"), "tensor"), P(("groups", "seq"), "tensor"))
    sizes = (mesh.shape["tensor"], mesh.shape["vocab"], mesh.shape["seq"])
    body = fused if sizes == (TENSOR, VOCAB, SEQ) else general
    return jax.shard_map(
        body, mesh=mesh, in_specs=in_specs, out_specs=out_specs, check_vma=False
    )
```
